32 devices in a mesh: seq: 4 (over x, core), shard: 8 (over z, y).
Axes of the slice: x: 2, y: 2, z: 4, core: 2. Of those that a mesh axis runs over, the one named last changes fastest.
Arguments:
- tokens: bfloat16 [8, 2048, 1024], P('shard', 'seq'), may hold values from -6 to 6
- cotangent: bfloat16 [8, 2048, 1024], P('shard', 'seq'), may hold values from -6 to 6
- entry_weight: float32 [1024, 3072], P(('seq', 'shard')), may hold values from -0.1875 to 0.1875
- entry_drift: float32 [1024, 3072], P(('seq', 'shard')), may hold values from -64 to 64
- entry_power: float32 [1024, 3072], P(('seq', 'shard')), may hold values from 8.192 to 32.768
- exit_weight: float32 [1024, 1024], P(('seq', 'shard')), may hold values from -6 to 6
- exit_drift: float32 [1024, 1024], P(('seq', 'shard')), may hold values from -4 to 4
- exit_power: float32 [1024, 1024], P(('seq', 'shard')), may hold values from 0.0064 to 0.0256
- expand_weight: float32 [1024, 4096], P(('seq', 'shard')), may hold values from -0.1875 to 0.1875
- expand_drift: float32 [1024, 4096], P(('seq', 'shard')), may hold values from -16 to 16
- expand_power: float32 [1024, 4096], P(('seq', 'shard')), may hold values from 0.65536 to 2.62144
- reduce_weight: float32 [4096, 1024], P(('seq', 'shard')), may hold values from -0.09375 to 0.09375
- reduce_drift: float32 [4096, 1024], P(('seq', 'shard')), may hold values from -40 to 40
- reduce_power: float32 [4096, 1024], P(('seq', 'shard')), may hold values from 3.2768 to 13.1072
- vectors: float32 [12, 1024], P(None, ('seq', 'shard')), may hold values from -1 to 1.3, as said below
- vectors_drift: float32 [12, 1024], P(None, ('seq', 'shard')), may hold values from -71.04 to 71.04, as said below
- vectors_power: float32 [12, 1024], P(None, ('seq', 'shard')), may hold values from 0.65536 to 65.536, as said below
Outputs:
- block_out: bfloat16 [8, 2048, 1024], P('shard', 'seq')
- input_grad: float32 [8, 2048, 1024], P('shard', 'seq')
- drift_entry: float32 [1024, 3072], P(('seq', 'shard'))
- power_entry: float32 [1024, 3072], P(('seq', 'shard'))
- moved_entry: float32 [1024, 3072], P(('seq', 'shard'))
- drift_exit: float32 [1024, 1024], P(('seq', 'shard'))
- power_exit: float32 [1024, 1024], P(('seq', 'shard'))
- moved_exit: float32 [1024, 1024], P(('seq', 'shard'))
- drift_expand: float32 [1024, 4096], P(('seq', 'shard'))
- power_expand: float32 [1024, 4096], P(('seq', 'shard'))
- moved_expand: float32 [1024, 4096], P(('seq', 'shard'))
- drift_reduce: float32 [4096, 1024], P(('seq', 'shard'))
- power_reduce: float32 [4096, 1024], P(('seq', 'shard'))
- moved_reduce: float32 [4096, 1024], P(('seq', 'shard'))
- drift_vectors: float32 [12, 1024], P(None, ('seq', 'shard'))
- power_vectors: float32 [12, 1024], P(None, ('seq', 'shard'))
- moved_vectors: float32 [12, 1024], P(None, ('seq', 'shard'))
The draws below stay inside these ranges and needn't reach their ends.
Inputs may be any that keep to these rules, and one draw needn't show every extreme that they name: `vectors`: rows 3 and 6 are gains near one, the others biases. `vectors_drift`: both signs. `vectors_power`: positive.
All inputs are finite; a program needn't handle non-finite values.
Results may differ from the reference program's by a relative error of at most 0.012.
The reference program's roundings to bfloat16 on the way count: a program that leaves them out, or rounds other values in their place, can miss the bound.
Values may be sent and summed in bfloat16 or wider, within the bound.
A program may use at most 192 MiB of HBM per device.

```python
import math
import jax
import jax.numpy as jnp
import numpy as np
from jax import lax

D = 1024
FF = 4096
HEADS = 16
HEAD_DIM = 64
QBLK = 512
STEP = 10
SEQ_LEN = 2048
SEQS = 8
TOKENS = 16384


ROW_GRAD = np.array([0.7, 0.7, 0.55, 0.8, 0.8, 0.7, 1.0, 1.0, 0.2, 0.2, 0.2, 0.2], np.float32)


def draw_vectors(key, part):
    key = jax.random.fold_in(key, 11)
    first_key, second_key = jax.random.split(key)
    shifts = 0.2 * jax.random.truncated_normal(first_key, -5.0, 5.0, (12, D), jnp.float32)
    gains = 1.0 + jax.random.uniform(second_key, (12, D), jnp.float32, -0.3, 0.3)
    rows_index = jnp.arange(12)
    is_gain = (rows_index == 3) | (rows_index == 6)
    return jnp.where(is_gain[:, None], gains, shifts)


def draw_vectors_drift(key, part):
    key = jax.random.fold_in(key, 12)
    scales = jnp.asarray(ROW_GRAD)[:, None] * (0.111 * TOKENS ** 0.5)
    return scales * jax.random.truncated_normal(key, -5.0, 5.0, (12, D), jnp.float32)


def draw_vectors_power(key, part):
    key = jax.random.fold_in(key, 13)
    factor = jnp.exp(jax.random.uniform(key, (12, D), jnp.float32, 0.0, math.log(4.0)))
    row_scale = jnp.asarray(ROW_GRAD)[:, None]
    return row_scale * row_scale * (0.001 * TOKENS) * factor


def shard_levels(own_key, dims, shards, low, high):
    level, own = 1.0, jax.random.fold_in(own_key, 6)
    for axis_at, parts in shards:
        heights = jnp.exp(jax.random.uniform(jax.random.fold_in(own, axis_at), (parts,), jnp.float32, low / len(shards), high / len(shards)))
        level = level * jnp.repeat(heights, dims[axis_at] // parts).reshape([-1 if axis == axis_at else 1 for axis in range(len(dims))])
    return level


def scatter_about(rng, shape, scale, most, pieces=(), held_as=jnp.bfloat16):
    values = scale * jax.random.normal(rng, shape, jnp.float32)
    if pieces:
        values = values * shard_levels(rng, shape, pieces, -0.22, 0.18)
    return jnp.clip(values, -most, most).astype(held_as)


def setup_inputs(seed: int = 0) -> dict:
    key_list = jax.random.split(jax.random.key(seed), 18)
    return {
        "tokens": scatter_about(key_list[0], (SEQS, SEQ_LEN, D), 1.0, 6.0, ((0, 8), (1, 4))),
        "cotangent": scatter_about(key_list[1], (SEQS, SEQ_LEN, D), 1.0, 6.0, ((0, 8), (1, 4))),
        "entry_weight": scatter_about(key_list[2], (D, 3 * D), D ** -0.5, 0.1875, ((0, 32),), jnp.float32),
        "entry_drift": scatter_about(key_list[3], (D, 3 * D), (0.078 * TOKENS ** 0.5), 64.0, ((0, 32),), jnp.float32),
        "entry_power": jnp.clip(jnp.exp(math.log(32.768) - 1.3862944 * jax.random.uniform(key_list[4], (D, 3 * D), jnp.float32) ** shard_levels(key_list[4], (D, 3 * D), ((0, 32),), -0.2, 0.2)), 8.192, 32.768),
        "exit_weight": scatter_about(key_list[5], (D, D), (max(1, 3 * D // SEQ_LEN)) ** -0.5, 6.0, ((0, 32),), jnp.float32),
        "exit_drift": scatter_about(key_list[6], (D, D), (0.1 * SEQS ** 0.5), 4.0, ((0, 32),), jnp.float32),
        "exit_power": jnp.clip(jnp.exp(math.log(0.0256) - 1.3862944 * jax.random.uniform(key_list[7], (D, D), jnp.float32) ** shard_levels(key_list[7], (D, D), ((0, 32),), -0.2, 0.2)), 0.0064, 0.0256),
        "expand_weight": scatter_about(key_list[8], (D, FF), D ** -0.5, 0.1875, ((0, 32),), jnp.float32),
        "expand_drift": scatter_about(key_list[9], (D, FF), (0.022 * TOKENS ** 0.5), 16.0, ((0, 32),), jnp.float32),
        "expand_power": jnp.clip(jnp.exp(math.log(2.62144) - 1.3862944 * jax.random.uniform(key_list[10], (D, FF), jnp.float32) ** shard_levels(key_list[10], (D, FF), ((0, 32),), -0.2, 0.2)), 0.65536, 2.62144),
        "reduce_weight": scatter_about(key_list[11], (FF, D), FF ** -0.5, 0.09375, ((0, 32),), jnp.float32),
        "reduce_drift": scatter_about(key_list[12], (FF, D), (0.05 * TOKENS ** 0.5), 40.0, ((0, 32),), jnp.float32),
        "reduce_power": jnp.clip(jnp.exp(math.log(13.1072) - 1.3862944 * jax.random.uniform(key_list[13], (FF, D), jnp.float32) ** shard_levels(key_list[13], (FF, D), ((0, 32),), -0.2, 0.2)), 3.2768, 13.1072),
        "vectors": draw_vectors(jax.random.fold_in(key_list[17], 71), 0),
        "vectors_drift": draw_vectors_drift(jax.random.fold_in(key_list[17], 71), 0),
        "vectors_power": draw_vectors_power(jax.random.fold_in(key_list[17], 71), 0),
    }


@jax.custom_vjp
def low(v):
    return lax.optimization_barrier(v.astype(jnp.bfloat16)).astype(jnp.float32)

@jax.custom_vjp
def low_back(v):
    return v

def low_keep(v):
    return (low(v), None)

def low_pass(kept, grad):
    return (grad,)

def back_keep(v):
    return (v, None)

def back_low(kept, grad):
    return (low(grad),)
low.defvjp(low_keep, low_pass)
low_back.defvjp(back_keep, back_low)
NORM_EPS = 1e-05
ADAM_EPS = 1e-06
DECAY_ONE = 0.9
DECAY_TWO = 0.999
HIGH = lax.Precision.HIGHEST

def product(left, right):
    return jnp.dot(left, right, precision=HIGH, preferred_element_type=jnp.float32)

def layer_norm(summed, gain_row, shift_row):
    centre = lax.optimization_barrier(jnp.mean(summed, axis=-1, keepdims=True))
    centred = summed - centre
    variance = lax.optimization_barrier(jnp.mean(centred * centred, axis=-1, keepdims=True))
    return centred * lax.rsqrt(variance + NORM_EPS) * gain_row + shift_row

def attention(queries, key_rows, value_rows):
    length = queries.shape[0]
    blocked = queries.reshape(length // QBLK, QBLK, HEADS, HEAD_DIM)

    def one_block(query_block):
        scores = low_back(jnp.einsum('qhd,khd->hqk', query_block, key_rows, precision=HIGH) * 0.125)
        highest = lax.optimization_barrier(jnp.max(scores, axis=-1, keepdims=True))
        exponent = jnp.exp(scores - highest)
        weights = exponent / lax.optimization_barrier(jnp.sum(exponent, axis=-1, keepdims=True))
        return jnp.einsum('hqk,khd->qhd', low(weights), value_rows, precision=HIGH)
    context = lax.map(jax.checkpoint(one_block), blocked)
    return context.reshape(length, HEADS * HEAD_DIM)

def forward(inputs, entry_weight, exit_weight, expand_weight, reduce_weight, vectors):
    entry_low = low(entry_weight)
    exit_low = low(exit_weight)
    expand_low = low(expand_weight)
    reduce_low = low(reduce_weight)
    vector_rows = low(vectors)
    length, width = inputs.shape
    bias_entry = jnp.concatenate([vector_rows[0], jnp.zeros((width,), jnp.float32), vector_rows[1]])
    projected = low_back(low(product(inputs, entry_low) + bias_entry))
    queries = projected[:, :width].reshape(length, HEADS, HEAD_DIM)
    key_rows = projected[:, width:2 * width].reshape(length, HEADS, HEAD_DIM)
    value_rows = projected[:, 2 * width:].reshape(length, HEADS, HEAD_DIM)
    context = low_back(low(attention(queries, key_rows, value_rows)))
    attended = low_back(product(context, exit_low) + vector_rows[2])
    mixed_rows = layer_norm(inputs + attended, vector_rows[3], vector_rows[4])
    pre_act = low_back(product(low(mixed_rows), expand_low) + vector_rows[8:].reshape(-1))
    activated = low(jax.nn.gelu(pre_act, approximate=False))
    branch = low_back(product(activated, reduce_low) + vector_rows[5])
    return layer_norm(mixed_rows + branch, vector_rows[6], vector_rows[7])

def adam_step(weight, drift_old, power_old, gradient, step_rate, decay_rate):
    drift_new = DECAY_ONE * drift_old + (1.0 - DECAY_ONE) * gradient
    power_new = DECAY_TWO * power_old + (1.0 - DECAY_TWO) * gradient * gradient
    normalized = drift_new / (1.0 - DECAY_ONE ** STEP) / (jnp.sqrt(power_new / (1.0 - DECAY_TWO ** STEP)) + ADAM_EPS)
    return (drift_new, power_new, weight - step_rate * (normalized + decay_rate * weight))

def reference(tokens, cotangent, entry_weight, entry_drift, entry_power, exit_weight, exit_drift, exit_power, expand_weight, expand_drift, expand_power, reduce_weight, reduce_drift, reduce_power, vectors, vectors_drift, vectors_power):
    masters = (entry_weight, exit_weight, expand_weight, reduce_weight, vectors)

    def one_sequence(running, pair):
        seq_tokens, seq_cotangent = pair
        result, pull = jax.vjp(forward, seq_tokens.astype(jnp.float32), entry_weight, exit_weight, expand_weight, reduce_weight, vectors)
        gradients = pull(seq_cotangent.astype(jnp.float32))
        running = tuple((total + gradient for total, gradient in zip(running, gradients[1:])))
        return (running, (result.astype(jnp.bfloat16), gradients[0]))
    start = tuple((jnp.zeros_like(master) for master in masters))
    totals, outputs = lax.scan(one_sequence, start, (tokens, cotangent))
    block_out, input_grad = outputs
    entry_new = adam_step(entry_weight, entry_drift, entry_power, totals[0], 0.03, 0.01)
    exit_new = adam_step(exit_weight, exit_drift, exit_power, totals[1], 0.3, 0.01)
    expand_new = adam_step(expand_weight, expand_drift, expand_power, totals[2], 0.03, 0.01)
    reduce_new = adam_step(reduce_weight, reduce_drift, reduce_power, totals[3], 0.02, 0.01)
    vectors_new = adam_step(vectors, vectors_drift, vectors_power, totals[4], 0.2, 0.0)
    return (block_out, input_grad, entry_new[0], entry_new[1], entry_new[2], exit_new[0], exit_new[1], exit_new[2], expand_new[0], expand_new[1], expand_new[2], reduce_new[0], reduce_new[1], reduce_new[2], vectors_new[0], vectors_new[1], vectors_new[2])
```

```python
import math

import jax
import jax.numpy as jnp
from jax import lax
from jax.experimental import pallas as pl
from jax.experimental.pallas import tpu as pltpu
from jax.sharding import PartitionSpec as P

HEAD_DIM = 64
QBLK = 256
VMEM_BYTES = 56 * 1024 * 1024
STEP = 10


NORM_EPS = 1e-05
ADAM_EPS = 1e-06
DECAY_ONE = 0.9
DECAY_TWO = 0.999


def norm_forward(summed, gain_row, shift_row):
    centre = jnp.mean(summed, axis=-1, keepdims=True)
    centred = summed - centre
    inverse = lax.rsqrt(jnp.mean(centred * centred, axis=-1, keepdims=True) + NORM_EPS)
    normed = centred * inverse
    return (normed * gain_row + shift_row, normed, inverse)


def norm_backward(upstream, normed, inverse, gain_row):
    gain_grad = jnp.sum(upstream * normed, axis=0)
    shift_grad = jnp.sum(upstream, axis=0)
    scaled = upstream * gain_row
    bracket = (
        scaled
        - jnp.mean(scaled, axis=-1, keepdims=True)
        - normed * jnp.mean(scaled * normed, axis=-1, keepdims=True)
    )
    return (inverse * bracket, gain_grad, shift_grad)


def dot_nt(left, right):
    return lax.dot_general(left, right, (((1,), (1,)), ((), ())), preferred_element_type=jnp.float32)


def dot_nn(left, right):
    return jnp.dot(left, right, preferred_element_type=jnp.float32)


def forward_kernel(q_ref, k_ref, vt_ref, out_ref, log_ref):
    heads = q_ref.shape[1] // HEAD_DIM
    parts = []
    for head in range(heads):
        cols = slice(head * HEAD_DIM, (head + 1) * HEAD_DIM)
        query = q_ref[:, cols] * jnp.bfloat16(0.125)
        scores = dot_nt(k_ref[:, cols], query)
        highest = jnp.max(scores, axis=0, keepdims=True)
        powers = jnp.exp(scores - highest)
        total = jnp.sum(powers, axis=0, keepdims=True)
        weights = (powers * (1.0 / total)).astype(jnp.bfloat16)
        parts.append(dot_nn(vt_ref[cols, :], weights))
        log_ref[head : head + 1, :] = highest + jnp.log(total)
    out_ref[...] = jnp.concatenate(parts, axis=0).T.astype(jnp.bfloat16)


def attend_forward(packed, slot_width):
    length = packed.shape[0]
    heads = slot_width // HEAD_DIM
    values_t = packed[:, 2 * slot_width :].T
    flops = 4 * length * length * slot_width
    return pl.pallas_call(
        forward_kernel,
        grid=(length // QBLK,),
        in_specs=[
            pl.BlockSpec((QBLK, slot_width), lambda i: (i, 0)),
            pl.BlockSpec((length, slot_width), lambda i: (0, 1)),
            pl.BlockSpec((slot_width, length), lambda i: (0, 0)),
        ],
        out_specs=[
            pl.BlockSpec((QBLK, slot_width), lambda i: (i, 0)),
            pl.BlockSpec((heads, QBLK), lambda i: (0, i)),
        ],
        out_shape=[
            jax.ShapeDtypeStruct((length, slot_width), jnp.bfloat16),
            jax.ShapeDtypeStruct((heads, length), jnp.float32),
        ],
        compiler_params=pltpu.CompilerParams(vmem_limit_bytes=VMEM_BYTES),
        cost_estimate=pl.CostEstimate(
            flops=4 * flops,
            bytes_accessed=8 * length * slot_width,
            transcendentals=heads * length * length,
        ),
    )(packed, packed, values_t)


def backward_kernel(q_ref, k_ref, v_ref, kt_ref, up_ref, log_ref, out_ref, key_sum, value_sum):
    step = pl.program_id(0)
    width = q_ref.shape[1]
    heads = width // HEAD_DIM

    @pl.when(step == 0)
    def _():
        key_sum[...] = jnp.zeros_like(key_sum)
        value_sum[...] = jnp.zeros_like(value_sum)

    parts = []
    for head in range(heads):
        cols = slice(head * HEAD_DIM, (head + 1) * HEAD_DIM)
        query = q_ref[:, cols] * jnp.bfloat16(0.125)
        upstream = up_ref[:, cols]
        scores = dot_nt(k_ref[:, cols], query)
        weights = jnp.exp(scores - log_ref[head : head + 1, :])
        weight_grad = dot_nt(v_ref[:, cols], upstream)
        value_sum[:, cols] += dot_nn(weights.astype(jnp.bfloat16), upstream)
        centre = jnp.sum(weights * weight_grad, axis=0, keepdims=True)
        score_grad = (weights * (weight_grad - centre)).astype(jnp.bfloat16)
        key_sum[:, cols] += dot_nn(score_grad, query)
        parts.append(dot_nn(kt_ref[cols, :], score_grad))
    query_grad = jnp.concatenate(parts, axis=0).T * 0.125
    rows = pl.ds(pl.multiple_of(step * QBLK, QBLK), QBLK)
    out_ref[rows, 0:width] = query_grad.astype(jnp.bfloat16)

    @pl.when(step == pl.num_programs(0) - 1)
    def _():
        out_ref[:, width : 2 * width] = key_sum[...].astype(jnp.bfloat16)
        out_ref[:, 2 * width : 3 * width] = value_sum[...].astype(jnp.bfloat16)


def attend_backward(packed, log_total, upstream, slot_width):
    length = packed.shape[0]
    heads = slot_width // HEAD_DIM
    keys_t = packed[:, slot_width : 2 * slot_width].T
    flops = 10 * length * length * slot_width
    return pl.pallas_call(
        backward_kernel,
        grid=(length // QBLK,),
        in_specs=[
            pl.BlockSpec((QBLK, slot_width), lambda i: (i, 0)),
            pl.BlockSpec((length, slot_width), lambda i: (0, 1)),
            pl.BlockSpec((length, slot_width), lambda i: (0, 2)),
            pl.BlockSpec((slot_width, length), lambda i: (0, 0)),
            pl.BlockSpec((QBLK, slot_width), lambda i: (i, 0)),
            pl.BlockSpec((heads, QBLK), lambda i: (0, i)),
        ],
        out_specs=pl.BlockSpec((length, 3 * slot_width), lambda i: (0, 0)),
        out_shape=jax.ShapeDtypeStruct((length, 3 * slot_width), jnp.bfloat16),
        scratch_shapes=[
            pltpu.VMEM((length, slot_width), jnp.float32),
            pltpu.VMEM((length, slot_width), jnp.float32),
        ],
        compiler_params=pltpu.CompilerParams(vmem_limit_bytes=VMEM_BYTES),
        cost_estimate=pl.CostEstimate(
            flops=4 * flops,
            bytes_accessed=16 * length * slot_width,
            transcendentals=heads * length * length,
        ),
    )(packed, packed, packed, keys_t, upstream, log_total)


def axis_bits(axis):
    count = lax.axis_size(axis)
    return [(axis, bit) for bit in range(count.bit_length() - 1)]


def swap_bit(tensor, axis, bit):
    pairs = [(i, i ^ (1 << bit)) for i in range(lax.axis_size(axis))]
    return lax.ppermute(tensor, axis, pairs)


class Scatter:
    def __init__(self, grad, order):
        names = axis_bits("seq")[::-1] + axis_bits("shard")[::-1]
        rows, cols = grad.shape
        owners = 2 ** len(names)
        self.left = names
        self.order = order
        self.wire = grad.dtype
        self.part = grad.reshape((2,) * len(names) + (rows // owners, cols))

    def stage(self):
        axis, bit = self.order[0]
        self.order = self.order[1:]
        dim = self.left.index((axis, bit))
        self.left = self.left[:dim] + self.left[dim + 1 :]
        mine = (lax.axis_index(axis) >> bit) & 1
        keep = lax.dynamic_index_in_dim(self.part, mine, dim, keepdims=False)
        send = lax.dynamic_index_in_dim(self.part, 1 - mine, dim, keepdims=False)
        total = keep.astype(jnp.float32) + swap_bit(send, axis, bit).astype(jnp.float32)
        self.part = total.astype(self.wire) if self.order else total

    def finish(self):
        while self.order:
            self.stage()
        return self.part


def gather_vectors(rows):
    held = rows[None]
    for axis, bit in axis_bits("shard") + axis_bits("seq"):
        other = swap_bit(held, axis, bit)
        high = ((lax.axis_index(axis) >> bit) & 1) == 1
        first = jnp.where(high, other, held)
        second = jnp.where(high, held, other)
        held = jnp.concatenate([first, second], axis=0)
    return jnp.moveaxis(held, 0, 1).reshape(rows.shape[0], -1)


def adam_step(weight, drift_old, power_old, gradient, step_rate, decay_rate):
    drift_new = DECAY_ONE * drift_old + (1.0 - DECAY_ONE) * gradient
    power_new = DECAY_TWO * power_old + (1.0 - DECAY_TWO) * gradient * gradient
    normalized = (
        drift_new
        / (1.0 - DECAY_ONE**STEP)
        / (jnp.sqrt(power_new / (1.0 - DECAY_TWO**STEP)) + ADAM_EPS)
    )
    return (drift_new, power_new, weight - step_rate * (normalized + decay_rate * weight))


def body(
    tokens,
    cotangent,
    entry_weight,
    entry_drift,
    entry_power,
    exit_weight,
    exit_drift,
    exit_power,
    expand_weight,
    expand_drift,
    expand_power,
    reduce_weight,
    reduce_drift,
    reduce_power,
    vectors,
    vectors_drift,
    vectors_power,
):
    entry_low, exit_low, expand_low, reduce_low, vector_low = (
        lax.all_gather(entry_weight.astype(jnp.bfloat16), ("seq", "shard"), axis=0, tiled=True),
        lax.all_gather(exit_weight.astype(jnp.bfloat16), ("seq", "shard"), axis=0, tiled=True),
        lax.all_gather(expand_weight.astype(jnp.bfloat16), ("seq", "shard"), axis=0, tiled=True),
        lax.all_gather(reduce_weight.astype(jnp.bfloat16), ("seq", "shard"), axis=0, tiled=True),
        gather_vectors(vectors.astype(jnp.bfloat16)),
    )
    vector_rows = vector_low.astype(jnp.float32)
    seq_count, local_len, width = tokens.shape
    assert seq_count == 1
    row_count = local_len
    groups = lax.axis_size("seq")
    slot_width = width // groups
    inputs = tokens.reshape(row_count, width)

    def to_slots(matrix, blocks):
        shaped = matrix.reshape(row_count, blocks, groups, slot_width)
        sent = jnp.transpose(shaped, (2, 0, 1, 3)).reshape(groups, row_count, blocks * slot_width)
        got = lax.all_to_all(sent, "seq", split_axis=0, concat_axis=0, tiled=True)
        return got.reshape(groups * row_count, blocks * slot_width)

    def from_slots(matrix, blocks):
        sent = matrix.reshape(groups, row_count, blocks * slot_width)
        got = lax.all_to_all(sent, "seq", split_axis=0, concat_axis=0, tiled=True)
        shaped = got.reshape(groups, row_count, blocks, slot_width)
        return jnp.transpose(shaped, (1, 2, 0, 3)).reshape(row_count, blocks * width)

    bias_entry = jnp.concatenate([vector_rows[0], jnp.zeros((width,), jnp.float32), vector_rows[1]])
    projected = (
        jnp.dot(inputs, entry_low, preferred_element_type=jnp.float32) + bias_entry
    ).astype(jnp.bfloat16)
    packed = to_slots(projected, 3)
    context_heads, log_total = attend_forward(packed, slot_width)
    context = from_slots(context_heads, 1)
    attended = jnp.dot(context, exit_low, preferred_element_type=jnp.float32) + vector_rows[2]
    first_sum = inputs.astype(jnp.float32) + attended
    mixed_rows, normed_one, inverse_one = norm_forward(first_sum, vector_rows[3], vector_rows[4])
    mixed_low = mixed_rows.astype(jnp.bfloat16)
    pre_act = jnp.dot(mixed_low, expand_low, preferred_element_type=jnp.float32) + vector_rows[
        8:
    ].reshape(-1)
    normal_cdf = 0.5 + 0.5 * lax.erf(pre_act * math.sqrt(0.5))
    slope = normal_cdf + pre_act * jnp.exp(-0.5 * pre_act * pre_act) * (1.0 / math.sqrt(2.0 * math.pi))
    act_low = (pre_act * normal_cdf).astype(jnp.bfloat16)
    branch = jnp.dot(act_low, reduce_low, preferred_element_type=jnp.float32) + vector_rows[5]
    second_sum = mixed_rows + branch
    result, normed_two, inverse_two = norm_forward(second_sum, vector_rows[6], vector_rows[7])
    block_out = result.astype(jnp.bfloat16).reshape(tokens.shape)
    upstream = cotangent.reshape(row_count, width).astype(jnp.float32)
    second_grad, gain_two, shift_two = norm_backward(
        upstream, normed_two, inverse_two, vector_rows[6]
    )
    branch_grad = second_grad.astype(jnp.bfloat16)
    across = [("seq", 0)] + axis_bits("seq")[1:] + axis_bits("shard")
    along = [("seq", 0)] + axis_bits("shard") + axis_bits("seq")[1:]
    reduce_grad = jnp.einsum(
        "rf,rd->fd", act_low, branch_grad, preferred_element_type=jnp.float32
    ).astype(jnp.bfloat16)
    reduce_grad, branch_grad = lax.optimization_barrier((reduce_grad, branch_grad))
    reduce_sum = Scatter(reduce_grad, across)
    reduce_sum.stage()
    branch_bias = jnp.sum(branch_grad.astype(jnp.float32), axis=0)
    act_grad = jnp.einsum("rd,fd->rf", branch_grad, reduce_low, preferred_element_type=jnp.float32)
    pre_grad = (act_grad * slope).astype(jnp.bfloat16)
    expand_grad = jnp.einsum(
        "rd,rf->df", mixed_low, pre_grad, preferred_element_type=jnp.float32
    ).astype(jnp.bfloat16)
    expand_grad, pre_grad = lax.optimization_barrier((expand_grad, pre_grad))
    expand_sum = Scatter(expand_grad, along)
    expand_sum.stage()
    expand_bias = jnp.sum(pre_grad.astype(jnp.float32), axis=0).reshape(4, width)
    mixed_grad = second_grad + jnp.einsum(
        "rf,df->rd", pre_grad, expand_low, preferred_element_type=jnp.float32
    )
    vector_back = jnp.concatenate(
        [branch_bias[None], gain_two[None], shift_two[None], expand_bias], axis=0
    )
    first_grad, gain_one, shift_one = norm_backward(
        mixed_grad, normed_one, inverse_one, vector_rows[3]
    )
    attended_grad = first_grad.astype(jnp.bfloat16)
    exit_grad = jnp.einsum(
        "rc,rd->cd", context, attended_grad, preferred_element_type=jnp.float32
    ).astype(jnp.bfloat16)
    exit_bias = jnp.sum(attended_grad.astype(jnp.float32), axis=0)
    context_grad = jnp.einsum(
        "rd,cd->rc", attended_grad, exit_low, preferred_element_type=jnp.float32
    ).astype(jnp.bfloat16)
    exit_sum = Scatter(exit_grad, across)
    exit_sum.stage()
    heads_grad = to_slots(context_grad, 1)
    heads_grad, reduce_sum.part, expand_sum.part, exit_sum.part = lax.optimization_barrier(
        (heads_grad, reduce_sum.part, expand_sum.part, exit_sum.part)
    )
    packed_grad = attend_backward(packed, log_total, heads_grad, slot_width)
    for running in (reduce_sum, expand_sum):
        running.stage()
    packed_grad, reduce_sum.part, expand_sum.part = lax.optimization_barrier(
        (packed_grad, reduce_sum.part, expand_sum.part)
    )
    entry_back = from_slots(packed_grad, 3)
    entry_grad = jnp.einsum(
        "rd,re->de", inputs, entry_back, preferred_element_type=jnp.float32
    ).astype(jnp.bfloat16)
    entry_grad, entry_back = lax.optimization_barrier((entry_grad, entry_back))
    half = entry_grad.shape[1] // 2
    entry_sums = (Scatter(entry_grad[:, :half], across), Scatter(entry_grad[:, half:], along))
    bias_sums = jnp.sum(entry_back.astype(jnp.float32), axis=0)
    input_grad = first_grad + jnp.einsum(
        "re,de->rd", entry_back, entry_low, preferred_element_type=jnp.float32
    )
    vector_front = jnp.stack(
        [bias_sums[:width], bias_sums[2 * width :], exit_bias, gain_one, shift_one], axis=0
    )
    vector_grad = jnp.concatenate([vector_front, vector_back], axis=0)
    owners = groups * lax.axis_size("shard")
    own_cols = width // owners
    vector_grad = vector_grad.reshape(-1, owners, own_cols)
    vector_grad = jnp.moveaxis(vector_grad, 0, 1).reshape(owners, -1)
    summed_vectors = Scatter(vector_grad, across).finish().reshape(-1, own_cols)
    summed_reduce = reduce_sum.finish()
    summed_expand = expand_sum.finish()
    summed_exit = exit_sum.finish()
    summed_entry = jnp.concatenate([running.finish() for running in entry_sums], axis=1)
    entry_new = adam_step(entry_weight, entry_drift, entry_power, summed_entry, 0.03, 0.01)
    exit_new = adam_step(exit_weight, exit_drift, exit_power, summed_exit, 0.3, 0.01)
    expand_new = adam_step(expand_weight, expand_drift, expand_power, summed_expand, 0.03, 0.01)
    reduce_new = adam_step(reduce_weight, reduce_drift, reduce_power, summed_reduce, 0.02, 0.01)
    vectors_new = adam_step(vectors, vectors_drift, vectors_power, summed_vectors, 0.2, 0.0)
    return (
        block_out,
        input_grad.reshape(tokens.shape),
        entry_new[0],
        entry_new[1],
        entry_new[2],
        exit_new[0],
        exit_new[1],
        exit_new[2],
        expand_new[0],
        expand_new[1],
        expand_new[2],
        reduce_new[0],
        reduce_new[1],
        reduce_new[2],
        vectors_new[0],
        vectors_new[1],
        vectors_new[2],
    )


def solution(mesh):
    in_specs = (
        P("shard", "seq", None),
        P("shard", "seq", None),
        P(("seq", "shard"), None),
        P(("seq", "shard"), None),
        P(("seq", "shard"), None),
        P(("seq", "shard"), None),
        P(("seq", "shard"), None),
        P(("seq", "shard"), None),
        P(("seq", "shard"), None),
        P(("seq", "shard"), None),
        P(("seq", "shard"), None),
        P(("seq", "shard"), None),
        P(("seq", "shard"), None),
        P(("seq", "shard"), None),
        P(None, ("seq", "shard")),
        P(None, ("seq", "shard")),
        P(None, ("seq", "shard")),
    )
    out_specs = (
        P("shard", "seq", None),
        P("shard", "seq", None),
        P(("seq", "shard"), None),
        P(("seq", "shard"), None),
        P(("seq", "shard"), None),
        P(("seq", "shard"), None),
        P(("seq", "shard"), None),
        P(("seq", "shard"), None),
        P(("seq", "shard"), None),
        P(("seq", "shard"), None),
        P(("seq", "shard"), None),
        P(("seq", "shard"), None),
        P(("seq", "shard"), None),
        P(("seq", "shard"), None),
        P(None, ("seq", "shard")),
        P(None, ("seq", "shard")),
        P(None, ("seq", "shard")),
    )
    return jax.shard_map(body, mesh=mesh, in_specs=in_specs, out_specs=out_specs, check_vma=False)
```
